32 devices in a mesh: fsdp: 8 (over z, core), dp: 4 (over y, x).
Axes of the slice: x: 2, y: 2, z: 4, core: 2. Of those that a mesh axis runs over, the one named last changes fastest.
Arguments:
- target_x: bfloat16 [512, 4096], P('dp'), may hold values from -6 to 6
- target_y: bfloat16 [512, 4096], P('dp'), may hold values from -6 to 6
- poison_x: bfloat16 [1024, 4096], P('dp'), may hold values from -6 to 6
- poison_y: bfloat16 [1024, 4096], P('dp'), may hold values from -6 to 6
- w_gate: bfloat16 [4096, 7168], P(None, 'fsdp'), as said below
- w_up: bfloat16 [4096, 7168], P(None, 'fsdp'), as said below
- w_down: bfloat16 [7168, 4096], P('fsdp'), may hold values from -0.0625 to 0.0625
Outputs:
- poison_step: float32 [1024, 4096], P('dp', 'fsdp')
- alignment: float32 [], replicated
The draws below stay inside these ranges and needn't reach their ends.
Inputs may be any that keep to these rules, and one draw needn't show every extreme that they name: `w_gate`: a weight matrix whose entries have mean 0 and a root mean square near 4096 ** -0.5. `w_up`: a weight matrix whose entries have mean 0 and a root mean square near 4096 ** -0.5.
All inputs are finite; a program needn't handle non-finite values.
Results may differ from the reference program's by a relative error of at most 0.02.
Values may be sent and summed in bfloat16 or wider, within the bound.
A program may use at most 192 MiB of HBM per device.

```python
import math
import jax
import jax.numpy as jnp
from jax import lax

D = 4096
FF = 7168
TGT_TOKENS = 512
POI_TOKENS = 1024
N_DP = 4


def rising_weight(key):
    rate = math.log(4.0)
    norm_factor = math.sqrt((math.exp(2.0 * rate) - 1.0) / (2.0 * rate))
    entries = jnp.clip(jax.random.normal(key, (D, FF), jnp.float32), -6.0, 6.0)
    position = jnp.arange(D, dtype=jnp.float32) / float(max(D - 1, 1))
    row_gain = jnp.exp(rate * position) / norm_factor
    return (entries * row_gain[:, None] * float(D) ** (-0.5)).astype(jnp.bfloat16)


def draw_w_gate(key, part):
    return rising_weight(jax.random.fold_in(key, 11))


def draw_w_up(key, part):
    return rising_weight(jax.random.fold_in(key, 23))


def shard_levels(own_key, extent, cuts, smallest, high):
    loudness = 1.0
    for dim, parts in cuts:
        heights = jax.random.uniform(jax.random.fold_in(jax.random.fold_in(own_key, 6), dim), (parts,), jnp.float32, smallest / len(cuts), high / len(cuts))
        loudness = loudness * jnp.repeat(jnp.exp(heights), extent[dim] // parts).reshape((-1,) + (1,) * (len(extent) - 1 - dim))
    return loudness


def scatter_about(rng, shape, deviation, limit, cuts=(), kind=jnp.bfloat16):
    result = deviation * jax.random.normal(rng, shape, jnp.float32)
    if cuts:
        result = result * shard_levels(rng, shape, cuts, -0.22, 0.18)
    return jnp.clip(result, -limit, limit).astype(kind)


def setup_inputs(seed: int = 0) -> dict:
    streams_of = jax.random.split(jax.random.key(seed), 8)
    return {
        "target_x": scatter_about(streams_of[0], (TGT_TOKENS, D), 1.0, 6.0, ((0, 4),)),
        "target_y": scatter_about(streams_of[1], (TGT_TOKENS, D), 1.0, 6.0, ((0, 4),)),
        "poison_x": scatter_about(streams_of[2], (POI_TOKENS, D), 1.0, 6.0, ((0, 4),)),
        "poison_y": scatter_about(streams_of[3], (POI_TOKENS, D), 1.0, 6.0, ((0, 4),)),
        "w_gate": draw_w_gate(jax.random.fold_in(streams_of[7], 71), 0),
        "w_up": draw_w_up(jax.random.fold_in(streams_of[7], 71), 0),
        "w_down": scatter_about(streams_of[6], (FF, D), FF ** -0.5, 0.0625, ((0, 8),)),
    }


EPSILON = 1e-06

def silu_parts(preact):
    sigma = jax.nn.sigmoid(preact)
    silu_val = preact * sigma
    slope = sigma * (1.0 + preact * (1.0 - sigma))
    curve = sigma * (1.0 - sigma) * (2.0 + preact * (1.0 - 2.0 * sigma))
    return (silu_val, slope, curve)

def matmul(left, right):
    return jnp.dot(left, right, preferred_element_type=jnp.float32)

def inner_rows(left, right):
    return lax.dot_general(left, right, (((0,), (0,)), ((), ())), preferred_element_type=jnp.float32)

def inner_cols(left, right):
    return lax.dot_general(left, right, (((1,), (1,)), ((), ())), preferred_element_type=jnp.float32)

def mlp_forward(inputs, w_gate, w_up, w_down):
    gate_pre = matmul(inputs, w_gate)
    upper = matmul(inputs, w_up)
    silu_val, slope, curve = silu_parts(gate_pre)
    hidden = (silu_val * upper).astype(jnp.bfloat16)
    return (upper, silu_val, slope, curve, hidden, matmul(hidden, w_down))

def backward(inputs, labels, output, upper, silu_val, slope, w_down, token_total):
    error = ((inputs.astype(jnp.float32) + output - labels.astype(jnp.float32)) / token_total).astype(jnp.bfloat16)
    back_hidden = inner_cols(error, w_down)
    gate_back = (back_hidden * upper * slope).astype(jnp.bfloat16)
    upper_back = (back_hidden * silu_val).astype(jnp.bfloat16)
    return (error, back_hidden, gate_back, upper_back)

def group_sums(inputs, error, hidden, gate_back, upper_back):
    group_rows = inputs.shape[0] // N_DP

    def add_group(group, running):
        offset = (group * group_rows).astype(jnp.int32)
        x_rows, e_rows, h_rows, g_rows, u_rows = [lax.dynamic_slice_in_dim(source, offset, group_rows, 0) for source in (inputs, error, hidden, gate_back, upper_back)]
        pieces = (inner_rows(x_rows, g_rows), inner_rows(x_rows, u_rows), inner_rows(e_rows, h_rows))
        return tuple((summed + lax.optimization_barrier(piece.astype(jnp.bfloat16)).astype(jnp.float32) for summed, piece in zip(running, pieces)))
    zeros = jnp.zeros((D, FF), jnp.float32)
    return lax.fori_loop(0, N_DP, add_group, (zeros, zeros, zeros))

def reference(target_x, target_y, poison_x, poison_y, w_gate, w_up, w_down):
    upper_tgt, silu_tgt, slope_tgt, curve_tgt, hidden_tgt, output_tgt = mlp_forward(target_x, w_gate, w_up, w_down)
    error_tgt, back_tgt, gback_tgt, uback_tgt = backward(target_x, target_y, output_tgt, upper_tgt, silu_tgt, slope_tgt, w_down, TGT_TOKENS)
    grad_tgt = group_sums(target_x, error_tgt, hidden_tgt, gback_tgt, uback_tgt)
    upper_poi, silu_poi, slope_poi, curve_poi, hidden_poi, output_poi = mlp_forward(poison_x, w_gate, w_up, w_down)
    error_poi, back_poi, gback_poi, uback_poi = backward(poison_x, poison_y, output_poi, upper_poi, silu_poi, slope_poi, w_down, POI_TOKENS)
    grad_poi = group_sums(poison_x, error_poi, hidden_poi, gback_poi, uback_poi)
    norm_tt = sum((jnp.sum(piece * piece) for piece in grad_tgt))
    norm_pp = sum((jnp.sum(piece * piece) for piece in grad_poi))
    cross_tp = sum((jnp.sum(first * second) for first, second in zip(grad_tgt, grad_poi)))
    length_tgt = jnp.sqrt(norm_tt + EPSILON)
    length_poi = jnp.sqrt(norm_pp + EPSILON)
    denom = length_tgt * length_poi
    alignment = 1.0 - cross_tp / denom
    coef_tgt = -1.0 / denom
    coef_poi = cross_tp / (denom * length_poi * length_poi)
    v_gate, v_upper, v_down = tuple(((coef_tgt * first + coef_poi * second).astype(jnp.bfloat16) for first, second in zip(grad_tgt, grad_poi)))
    tan_gate = matmul(poison_x, v_gate)
    tan_upper = matmul(poison_x, v_upper)
    hidden_tan = (slope_poi * tan_gate * upper_poi + silu_poi * tan_upper).astype(jnp.bfloat16)
    output_tan = matmul(hidden_tan, w_down) + inner_cols(hidden_poi, v_down)
    back_tan = (output_tan / POI_TOKENS).astype(jnp.bfloat16)
    mixed = inner_cols(back_tan, w_down) + matmul(error_poi, v_down)
    gate_total = (mixed * upper_poi * slope_poi + back_poi * (curve_poi * tan_gate * upper_poi + slope_poi * tan_upper)).astype(jnp.bfloat16)
    upper_total = (mixed * silu_poi + back_poi * slope_poi * tan_gate).astype(jnp.bfloat16)
    gate_dir = (back_poi * slope_poi * upper_poi).astype(jnp.bfloat16)
    upper_dir = (back_poi * silu_poi).astype(jnp.bfloat16)
    input_grad = inner_cols(gate_total, w_gate) + inner_cols(upper_total, w_up) + inner_cols(gate_dir, v_gate) + inner_cols(upper_dir, v_upper) + back_tan.astype(jnp.float32)
    scaled = input_grad * float(POI_TOKENS * D)
    mean_sq = jnp.mean(scaled * scaled)
    return (scaled * lax.rsqrt(mean_sq + EPSILON), alignment)
```

```python
import jax
import jax.numpy as jnp
from jax import lax
from jax.sharding import PartitionSpec as P

EPSILON = 1e-06
BF = jnp.bfloat16
F32 = jnp.float32


def silu_parts(preact):
    sigma = jax.nn.sigmoid(preact)
    silu_val = preact * sigma
    slope = sigma * (1.0 + preact * (1.0 - sigma))
    curve = sigma * (1.0 - sigma) * (2.0 + preact * (1.0 - 2.0 * sigma))
    return (silu_val, slope, curve)


def matmul(left, right):
    return jnp.dot(left, right, preferred_element_type=F32)


def inner_cols(left, right):
    return lax.dot_general(
        left, right, (((1,), (1,)), ((), ())), preferred_element_type=F32
    )


def local(target_x, target_y, poison_x, poison_y, w_gate, w_up, w_down):
    model_width = w_gate.shape[0]
    hidden_width = w_gate.shape[1]
    n_dp = lax.axis_size("dp")
    n_fsdp = lax.axis_size("fsdp")
    n_tgt = target_x.shape[0]
    n_poi = poison_x.shape[0]
    n_row = n_tgt + n_poi
    tgt_total = n_tgt * n_dp
    poi_total = n_poi * n_dp
    columns = model_width // n_fsdp
    first = lax.axis_index("fsdp") * columns

    def own_cols(rows):
        return lax.dynamic_slice_in_dim(rows, first, columns, 1)

    def gather_rows(rows):
        return lax.all_gather(rows, "dp", axis=0, tiled=True)

    is_tgt_loc = jnp.arange(n_row) < n_tgt
    is_tgt_all = (jnp.arange(n_row * n_dp) % n_row) < n_tgt

    rows = jnp.concatenate([target_x, poison_x], axis=0)
    row_cols = own_cols(rows)
    all_cols = gather_rows(row_cols)
    gram_x = lax.psum(inner_cols(row_cols, all_cols).astype(BF), "fsdp")

    gate_pre = matmul(rows, w_gate)
    upper = matmul(rows, w_up)
    silu_val, slope, curve = silu_parts(gate_pre)
    hidden = (silu_val * upper).astype(BF)
    part_out = matmul(hidden, w_down).astype(BF)
    out_cols = lax.psum_scatter(part_out, "fsdp", scatter_dimension=1, tiled=True)
    hidden_all = gather_rows(hidden)
    gram_h_part, gram_x = lax.optimization_barrier(
        (inner_cols(hidden, hidden_all).astype(BF), gram_x)
    )
    gram_h = lax.psum(gram_h_part, "fsdp")

    goal_cols = own_cols(jnp.concatenate([target_y, poison_y], axis=0))
    share = jnp.where(is_tgt_loc, 1.0 / tgt_total, 1.0 / poi_total)[:, None]
    error_cols = (
        (row_cols.astype(F32) + out_cols.astype(F32) - goal_cols.astype(F32)) * share
    ).astype(BF)
    error = lax.all_gather(error_cols, "fsdp", axis=1, tiled=True)
    error_all = gather_rows(error_cols)
    gram_e_part = inner_cols(error_cols, error_all)
    gram_e_own, gram_h = lax.optimization_barrier((gram_e_part[n_tgt:].astype(BF), gram_h))
    gram_e = lax.psum(gram_e_own, "fsdp")
    back = inner_cols(error, w_down)
    back_both = jnp.concatenate([back * upper * slope, back * silu_val], axis=1).astype(BF)
    back_all = gather_rows(back_both)
    gram_b_part = inner_cols(back_both, back_all)
    gram_b_own, gram_e = lax.optimization_barrier((gram_b_part[n_tgt:].astype(BF), gram_e))
    gram_b = lax.psum(gram_b_own, "fsdp")

    both = gram_x.astype(F32) * gram_b_part + gram_h.astype(F32) * gram_e_part
    tgt_cols = jnp.where(is_tgt_all[None, :], both, 0.0)
    sum_tgt = jnp.sum(tgt_cols, axis=1)
    sum_all = jnp.sum(both, axis=1)
    sums = jnp.stack(
        [
            jnp.sum(sum_tgt[:n_tgt]),
            jnp.sum(sum_all[n_tgt:] - sum_tgt[n_tgt:]),
            jnp.sum(sum_tgt[n_tgt:]),
        ]
    )
    sums = lax.psum(sums, ("fsdp", "dp"))
    norm_tt, norm_pp, cross_tp = sums[0], sums[1], sums[2]
    length_tgt = jnp.sqrt(norm_tt + EPSILON)
    length_poi = jnp.sqrt(norm_pp + EPSILON)
    denom = length_tgt * length_poi
    alignment = 1.0 - cross_tp / denom
    coef_tgt = -1.0 / denom
    coef_poi = cross_tp / (denom * length_poi * length_poi)
    coef = jnp.where(is_tgt_all, coef_tgt, coef_poi)[None, :]

    def weigh(gram):
        return (gram.astype(F32) * coef).astype(BF)

    u_poi, s_poi = upper[n_tgt:], silu_val[n_tgt:]
    s1_poi, s2_poi = slope[n_tgt:], curve[n_tgt:]
    b_poi = back[n_tgt:]
    tangents = matmul(weigh(gram_x[n_tgt:]), back_all)
    tan_gate = tangents[:, :hidden_width]
    tan_upper = tangents[:, hidden_width:]
    hidden_tan = (s1_poi * tan_gate * u_poi + s_poi * tan_upper).astype(BF)
    tan_cols = lax.psum_scatter(
        matmul(hidden_tan, w_down).astype(BF), "fsdp", scatter_dimension=1, tiled=True
    ).astype(F32) + matmul(weigh(gram_h[n_tgt:]), error_all)
    back_tan_cols = (tan_cols * (1.0 / poi_total)).astype(BF)
    back_tan = lax.all_gather(back_tan_cols, "fsdp", axis=1, tiled=True)
    mixed = inner_cols(back_tan, w_down) + matmul(weigh(gram_e), hidden_all)
    gate_total = (
        mixed * u_poi * s1_poi + b_poi * (s2_poi * tan_gate * u_poi + s1_poi * tan_upper)
    ).astype(BF)
    upper_total = (mixed * s_poi + b_poi * s1_poi * tan_gate).astype(BF)
    part_grad = inner_cols(gate_total, w_gate) + inner_cols(upper_total, w_up)
    grad_cols = lax.psum_scatter(
        part_grad.astype(BF), "fsdp", scatter_dimension=1, tiled=True
    ).astype(F32)
    grad_cols = grad_cols + matmul(weigh(gram_b), all_cols) + back_tan_cols.astype(F32)
    scaled = grad_cols * float(poi_total * model_width)
    total_sq = lax.psum(jnp.sum(scaled * scaled), ("fsdp", "dp"))
    mean_sq = total_sq / float(poi_total * model_width)
    return (scaled * lax.rsqrt(mean_sq + EPSILON), alignment)


def solution(mesh):
    in_specs = (
        P("dp", None),
        P("dp", None),
        P("dp", None),
        P("dp", None),
        P(None, "fsdp"),
        P(None, "fsdp"),
        P("fsdp", None),
    )
    out_specs = (P("dp", "fsdp"), P())
    return jax.shard_map(local, mesh=mesh, in_specs=in_specs, out_specs=out_specs, check_vma=False)
```

```python
import functools
import jax
import jax.numpy as jnp
from jax import lax
from jax.experimental import pallas as pl
from jax.experimental.pallas import tpu as pltpu
from jax.sharding import PartitionSpec as P

EPSILON = 1e-06
BF = jnp.bfloat16
F32 = jnp.float32

MESH = pl.DeviceIdType.MESH
STEP = 16


def columns_of(width):
    return lambda ref, i: ref.at[:, pl.ds(pl.multiple_of(i * width, width), width)]


def rows_of(height):
    return lambda ref, i: ref.at[pl.ds(pl.multiple_of(i * height, height), height)]


def over_rows(count, body, init=0):
    return lax.fori_loop(
        0, count // STEP, lambda i, c: body(pl.ds(pl.multiple_of(i * STEP, STEP), STEP), i, c), init
    )


class Exchange:
    def __init__(self, n_fsdp, n_dp, send, recv, local_sem):
        self.n, self.n_dp, self.groups = n_fsdp, n_dp, n_fsdp // 2
        self.send, self.recv, self.local_sem = send, recv, local_sem
        self.count, self.local_count = 0, 0
        self.open, self.local_open = [], []
        self.me = lax.axis_index("fsdp")
        self.row = lax.axis_index("dp")
        self.core = lax.rem(self.me, 2)
        self.group = lax.div(self.me, 2)
        self.twin = {"fsdp": 2 * self.group + 1 - self.core}

    def ahead(self, k):
        return lax.rem(self.group + k, self.groups)

    def behind(self, k):
        return lax.rem(self.group + self.groups - k, self.groups)

    def peer(self, k):
        return {"fsdp": 2 * self.ahead(k) + self.core}

    def dp_peer(self, k):
        return {"dp": lax.rem(self.row + k, self.n_dp)}

    def greet(self, fsdp, dp, every=False):
        targets = []
        if every:
            targets += [{"fsdp": lax.rem(self.me + k, self.n)} for k in range(1, self.n)]
        elif fsdp:
            targets += [self.twin] + [self.peer(k) for k in range(1, self.groups)]
        if dp:
            targets += [self.dp_peer(k) for k in range(1, self.n_dp)]
        barrier = pltpu.get_barrier_semaphore()
        for device in targets:
            pl.semaphore_signal(barrier, inc=1, device_id=device, device_id_type=MESH)
        pl.semaphore_wait(barrier, len(targets))

    def start(self, src, dst, device):
        copy = pltpu.make_async_remote_copy(
            src_ref=src,
            dst_ref=dst,
            send_sem=self.send.at[self.count],
            recv_sem=self.recv.at[self.count],
            device_id=device,
            device_id_type=MESH,
        )
        copy.start()
        self.count += 1
        self.open.append(copy)
        return copy

    def keep(self, src, dst):
        copy = pltpu.make_async_copy(src, dst, self.local_sem.at[self.local_count])
        copy.start()
        self.local_count += 1
        self.local_open.append(copy)

    def finish(self):
        for copy in self.open:
            copy.wait_send()
        for copy in self.local_open:
            copy.wait()

    def dp_gather(self, src, dst):
        height = src.shape[0]
        own = dst.at[pl.ds(pl.multiple_of(self.row * height, height), height)]
        self.keep(src, own)
        return [self.start(src, own, self.dp_peer(k)) for k in range(1, self.n_dp)]

    def reduce_open(self, part, piece, twin_buf):
        order = list(range(1, self.groups)) + [0]
        return {
            k: self.start(
                piece(part, 2 * self.ahead(k) + 1 - self.core), twin_buf.at[k], self.twin
            )
            for k in order
        }

    def reduce_send(self, part, piece, twin_buf, half, far_buf, opened):
        sent = []
        for k in range(1, self.groups):
            mine = piece(part, 2 * self.ahead(k) + self.core)
            opened[k].wait_recv()

            def add(rows, i, c, mine=mine, k=k):
                half[k - 1, rows, :] = (
                    mine[rows, :].astype(F32) + twin_buf[k, rows, :].astype(F32)
                ).astype(BF)
                return c

            over_rows(half.shape[1], add)
            sent.append(self.start(half.at[k - 1], far_buf.at[k - 1], self.peer(k)))
        return sent

    def reduce_close(self, part, piece, twin_buf, far_buf, opened, sent):
        opened[0].wait_recv()
        for copy in sent:
            copy.wait_recv()
        mine = piece(part, self.me)

        def total(rows):
            value = mine[rows, :].astype(F32) + twin_buf[0, rows, :].astype(F32)
            for k in range(1, self.groups):
                value = value + far_buf[k - 1, rows, :].astype(F32)
            return value

        return total

    def spread_open(self, own, full, piece):
        target = piece(full, self.me)
        self.keep(own, target)
        far = [self.start(own, target, self.peer(k)) for k in range(1, self.groups)]
        return far, [self.start(own, target, self.twin)]

    def spread_close(self, full, piece, far, near):
        for k in range(1, self.groups):
            far[k - 1].wait_recv()
            block = piece(full, 2 * self.behind(k) + self.core)
            near.append(self.start(block, block, self.twin))
        for copy in near:
            copy.wait_recv()

    def sum_tiles(self, tiles, row_tiles):
        copies = [
            self.start(
                tiles.at[self.me], tiles.at[self.me], {"fsdp": lax.rem(self.me + k, self.n)}
            )
            for k in range(1, self.n)
        ]
        for copy in copies:
            copy.wait_recv()
        value = tiles[0]
        for j in range(1, self.n):
            value = value + tiles[j]
        row_tiles[self.row] = value
        copies = [
            self.start(row_tiles.at[self.row], row_tiles.at[self.row], self.dp_peer(k))
            for k in range(1, self.n_dp)
        ]
        for copy in copies:
            copy.wait_recv()
        value = row_tiles[0]
        for j in range(1, self.n_dp):
            value = value + row_tiles[j]
        return value


def reduce_scratch(n, height, width):
    g = n // 2
    return [
        pltpu.VMEM((g, height, width), BF),
        pltpu.VMEM((g - 1, height, width), BF),
        pltpu.VMEM((g - 1, height, width), BF),
    ]


def communicate(body, n, n_dp, copies, kept, outs, ins, scratch, ident, flops=0):
    sems = [
        pltpu.SemaphoreType.DMA((copies,)),
        pltpu.SemaphoreType.DMA((copies,)),
        pltpu.SemaphoreType.DMA((max(kept, 1),)),
    ]

    def kernel(*refs):
        ex = Exchange(n, n_dp, refs[-3], refs[-2], refs[-1])
        body(ex, *refs[:-3])
        ex.finish()
        assert ex.count == copies and ex.local_count == kept, (ex.count, ex.local_count)

    vmem = pl.BlockSpec(memory_space=pltpu.VMEM)
    anyw = pl.BlockSpec(memory_space=pl.ANY)
    return pl.pallas_call(
        kernel,
        out_shape=[jax.ShapeDtypeStruct(shape, kind) for shape, kind, _ in outs],
        in_specs=[vmem if v else anyw for _, v in ins],
        out_specs=[vmem if v else anyw for _, _, v in outs],
        scratch_shapes=list(scratch) + sems,
        compiler_params=pltpu.CompilerParams(
            collective_id=ident, has_side_effects=True, vmem_limit_bytes=40 * 1024 * 1024
        ),
    )(*[a for a, _ in ins])


def forward_exchange(n, n_dp, n_tgt, part, row_cols, goal_cols, hidden):
    height, width = row_cols.shape
    piece = columns_of(width)
    tgt_share, poi_share = 1.0 / (n_tgt * n_dp), 1.0 / ((height - n_tgt) * n_dp)

    def body(ex, part, x, goal, hidden, error, own, all_x, all_h, all_e, twin, half, far):
        ex.greet(True, True)
        opened = ex.reduce_open(part, piece, twin)
        gathers = ex.dp_gather(x, all_x) + ex.dp_gather(hidden, all_h)
        sent = ex.reduce_send(part, piece, twin, half, far, opened)
        total = ex.reduce_close(part, piece, twin, far, opened, sent)

        def loss(rows, i, c):
            share = jnp.where(i * STEP < n_tgt, tgt_share, poi_share)
            value = x[rows, :].astype(F32) + total(rows) - goal[rows, :].astype(F32)
            own[rows, :] = (value * share).astype(BF)
            return c

        over_rows(height, loss)
        spread = ex.spread_open(own, error, piece)
        gathers += ex.dp_gather(own, all_e)
        ex.spread_close(error, piece, *spread)
        for copy in gathers:
            copy.wait_recv()

    g = n // 2
    return communicate(
        body, n, n_dp, g + (g - 1) + (g - 1) + g + 3 * (n_dp - 1), 4,
        [
            ((height, width * n), BF, True),
            ((height, width), BF, True),
            ((height * n_dp, width), BF, False),
            ((height * n_dp, hidden.shape[1]), BF, False),
            ((height * n_dp, width), BF, False),
        ],
        [(part, True), (row_cols, True), (goal_cols, True), (hidden, False)],
        reduce_scratch(n, height, width), 1,
    )


def gram_exchange(n, n_dp, grams, back_both):
    height, width = grams.shape
    piece = rows_of(height // n)

    def body(ex, grams, back, summed, all_b, own, twin, half, far):
        ex.greet(True, True)
        opened = ex.reduce_open(grams, piece, twin)
        gathers = ex.dp_gather(back, all_b)
        sent = ex.reduce_send(grams, piece, twin, half, far, opened)
        total = ex.reduce_close(grams, piece, twin, far, opened, sent)

        def store(rows, i, c):
            own[rows, :] = total(rows).astype(BF)
            return c

        over_rows(height // n, store)
        ex.spread_close(summed, piece, *ex.spread_open(own, summed, piece))
        for copy in gathers:
            copy.wait_recv()

    g = n // 2
    return communicate(
        body, n, n_dp, g + (g - 1) + (g - 1) + g + (n_dp - 1), 2,
        [
            ((height, width), BF, True),
            ((back_both.shape[0] * n_dp, back_both.shape[1]), BF, False),
        ],
        [(grams, True), (back_both, False)],
        [pltpu.VMEM((height // n, width), BF)] + reduce_scratch(n, height // n, width), 2,
    )


def sum_exchange(n, n_dp, tile):
    def body(ex, tile, out, tiles, row_tiles):
        ex.greet(True, True, every=True)
        tiles[ex.me] = tile[...]
        out[...] = ex.sum_tiles(tiles, row_tiles)

    return communicate(
        body, n, n_dp, (n - 1) + (n_dp - 1), 0,
        [(tile.shape, F32, True)],
        [(tile, True)],
        [pltpu.VMEM((n,) + tile.shape, F32), pltpu.VMEM((n_dp,) + tile.shape, F32)], 3,
    )[0]


def tangent_exchange(n, n_dp, poi_total, part, extra, gram):
    height, width = extra.shape
    piece = columns_of(width)
    low = gram.shape[0] // n
    low_piece = rows_of(low)

    def body(ex, part, extra, gram, full, own, summed, low_own, t1, h1, f1, t2, h2, f2):
        ex.greet(True, False)
        opened = ex.reduce_open(part, piece, t1)
        low_opened = ex.reduce_open(gram, low_piece, t2)
        sent = ex.reduce_send(part, piece, t1, h1, f1, opened)
        low_sent = ex.reduce_send(gram, low_piece, t2, h2, f2, low_opened)
        total = ex.reduce_close(part, piece, t1, f1, opened, sent)

        def store(rows, i, c):
            own[rows, :] = ((total(rows) + extra[rows, :]) * (1.0 / poi_total)).astype(BF)
            return c

        over_rows(height, store)
        spread = ex.spread_open(own, full, piece)
        low_total = ex.reduce_close(gram, low_piece, t2, f2, low_opened, low_sent)

        def low_store(rows, i, c):
            low_own[rows, :] = low_total(rows).astype(BF)
            return c

        over_rows(low, low_store)
        low_spread = ex.spread_open(low_own, summed, low_piece)
        ex.spread_close(full, piece, *spread)
        ex.spread_close(summed, low_piece, *low_spread)

    g = n // 2
    return communicate(
        body, n, n_dp, 2 * (g + (g - 1) + (g - 1) + g), 2,
        [((height, width * n), BF, True), ((height, width), BF, True), (gram.shape, BF, True)],
        [(part, True), (extra, True), (gram, True)],
        [pltpu.VMEM((low, gram.shape[1]), BF)]
        + reduce_scratch(n, height, width)
        + reduce_scratch(n, low, gram.shape[1]), 4,
    )


def final_exchange(n, n_dp, scale, entries, part, extra):
    height, width = extra.shape
    piece = columns_of(width)

    def body(ex, part, extra, out, twin, half, far, tiles, row_tiles):
        ex.greet(True, True, every=True)
        opened = ex.reduce_open(part, piece, twin)
        sent = ex.reduce_send(part, piece, twin, half, far, opened)
        total = ex.reduce_close(part, piece, twin, far, opened, sent)

        def store(rows, i, c):
            value = (total(rows) + extra[rows, :]) * scale
            out[rows, :] = value
            return c + value * value

        squares = over_rows(height, store, jnp.zeros((STEP, width), F32))
        tiles[ex.me] = jnp.broadcast_to(jnp.sum(squares), (8, 128))
        summed = ex.sum_tiles(tiles, row_tiles)
        factor = lax.rsqrt(jnp.max(summed) / entries + EPSILON)

        def rescale(rows, i, c):
            out[rows, :] = out[rows, :] * factor
            return c

        over_rows(height, rescale)

    g = n // 2
    return communicate(
        body, n, n_dp, g + (g - 1) + (n - 1) + (n_dp - 1), 0,
        [((height, width), F32, True)],
        [(part, True), (extra, True)],
        reduce_scratch(n, height, width)
        + [pltpu.VMEM((n, 8, 128), F32), pltpu.VMEM((n_dp, 8, 128), F32)], 5,
    )[0]


def silu_parts(preact):
    sigma = jax.nn.sigmoid(preact)
    silu_val = preact * sigma
    slope = sigma * (1.0 + preact * (1.0 - sigma))
    curve = sigma * (1.0 - sigma) * (2.0 + preact * (1.0 - 2.0 * sigma))
    return (silu_val, slope, curve)


def matmul(left, right):
    return jnp.dot(left, right, preferred_element_type=F32)


def inner_cols(left, right):
    return lax.dot_general(
        left, right, (((1,), (1,)), ((), ())), preferred_element_type=F32
    )


def local(target_x, target_y, poison_x, poison_y, w_gate, w_up, w_down):
    model_width = w_gate.shape[0]
    hidden_width = w_gate.shape[1]
    n_dp = lax.axis_size("dp")
    n_fsdp = lax.axis_size("fsdp")
    n_tgt = target_x.shape[0]
    n_poi = poison_x.shape[0]
    n_row = n_tgt + n_poi
    tgt_total = n_tgt * n_dp
    poi_total = n_poi * n_dp
    columns = model_width // n_fsdp
    first = lax.axis_index("fsdp") * columns

    def own_cols(rows):
        return lax.dynamic_slice_in_dim(rows, first, columns, 1)

    is_tgt_all = (jnp.arange(n_row * n_dp) % n_row) < n_tgt

    rows = jnp.concatenate([target_x, poison_x], axis=0)
    row_cols = own_cols(rows)
    goal_cols = jnp.concatenate([own_cols(target_y), own_cols(poison_y)], axis=0)

    gate_pre = matmul(rows, w_gate)
    upper = matmul(rows, w_up)
    silu_val, slope, curve = silu_parts(gate_pre)
    hidden = (silu_val * upper).astype(BF)
    part_out = matmul(hidden, w_down).astype(BF)
    error, error_cols, all_cols, hidden_all, error_all = forward_exchange(
        n_fsdp, n_dp, n_tgt, part_out, row_cols, goal_cols, hidden
    )

    back = inner_cols(error, w_down)
    back_both = jnp.concatenate([back * upper * slope, back * silu_val], axis=1).astype(BF)
    gram_e_part = inner_cols(error_cols, error_all)
    grams, back_all = gram_exchange(
        n_fsdp,
        n_dp,
        jnp.concatenate(
            [
                inner_cols(row_cols, all_cols).astype(BF),
                inner_cols(hidden, hidden_all).astype(BF),
                gram_e_part[n_tgt:].astype(BF),
            ],
            axis=0,
        ),
        back_both,
    )
    gram_x, gram_h, gram_e = grams[:n_row], grams[n_row : 2 * n_row], grams[2 * n_row :]
    gram_b_part = inner_cols(back_both, back_all)

    both = gram_x.astype(F32) * gram_b_part + gram_h.astype(F32) * gram_e_part
    sum_tgt = jnp.sum(jnp.where(is_tgt_all[None, :], both, 0.0), axis=1)
    sum_poi = jnp.sum(jnp.where(is_tgt_all[None, :], 0.0, both), axis=1)
    sums = jnp.stack(
        [jnp.sum(sum_tgt[:n_tgt]), jnp.sum(sum_poi[n_tgt:]), jnp.sum(sum_tgt[n_tgt:])]
    )
    tile = jnp.broadcast_to(jnp.pad(sums, (0, 5))[:, None], (8, 128))
    sums = sum_exchange(n_fsdp, n_dp, tile)[:, 0]
    norm_tt, norm_pp, cross_tp = sums[0], sums[1], sums[2]
    length_tgt = jnp.sqrt(norm_tt + EPSILON)
    length_poi = jnp.sqrt(norm_pp + EPSILON)
    denom = length_tgt * length_poi
    alignment = 1.0 - cross_tp / denom
    coef_tgt = -1.0 / denom
    coef_poi = cross_tp / (denom * length_poi * length_poi)
    coef = jnp.where(is_tgt_all, coef_tgt, coef_poi)[None, :]

    def weigh(gram):
        return (gram.astype(F32) * coef).astype(BF)

    u_poi, s_poi = upper[n_tgt:], silu_val[n_tgt:]
    s1_poi, s2_poi = slope[n_tgt:], curve[n_tgt:]
    b_poi = back[n_tgt:]
    tangents = matmul(weigh(gram_x[n_tgt:]), back_all)
    tan_gate = tangents[:, :hidden_width]
    tan_upper = tangents[:, hidden_width:]
    hidden_tan = (s1_poi * tan_gate * u_poi + s_poi * tan_upper).astype(BF)
    back_tan, back_tan_cols, gram_b = tangent_exchange(
        n_fsdp,
        n_dp,
        poi_total,
        matmul(hidden_tan, w_down).astype(BF),
        matmul(weigh(gram_h[n_tgt:]), error_all),
        gram_b_part[n_tgt:].astype(BF),
    )
    mixed = inner_cols(back_tan, w_down) + matmul(weigh(gram_e), hidden_all)
    gate_total = (
        mixed * u_poi * s1_poi + b_poi * (s2_poi * tan_gate * u_poi + s1_poi * tan_upper)
    ).astype(BF)
    upper_total = (mixed * s_poi + b_poi * s1_poi * tan_gate).astype(BF)
    part_grad = inner_cols(gate_total, w_gate) + inner_cols(upper_total, w_up)
    step = final_exchange(
        n_fsdp,
        n_dp,
        float(poi_total * model_width),
        float(poi_total * model_width),
        part_grad.astype(BF),
        matmul(weigh(gram_b), all_cols) + back_tan_cols.astype(F32),
    )
    return (step, alignment)


def solution(mesh):
    in_specs = (
        P("dp", None),
        P("dp", None),
        P("dp", None),
        P("dp", None),
        P(None, "fsdp"),
        P(None, "fsdp"),
        P("fsdp", None),
    )
    out_specs = (P("dp", "fsdp"), P())
    return jax.shard_map(local, mesh=mesh, in_specs=in_specs, out_specs=out_specs, check_vma=False)
```

```python
import functools
import jax
import jax.numpy as jnp
from jax import lax
from jax.experimental import pallas as pl
from jax.experimental.pallas import tpu as pltpu
from jax.sharding import PartitionSpec as P

EPSILON = 1e-06
BF = jnp.bfloat16
F32 = jnp.float32

MESH = pl.DeviceIdType.MESH
STEP = 16


def columns_of(width):
    return lambda ref, i: ref.at[:, pl.ds(pl.multiple_of(i * width, width), width)]


def rows_of(height):
    return lambda ref, i: ref.at[pl.ds(pl.multiple_of(i * height, height), height)]


def over_rows(count, body, init=0):
    return lax.fori_loop(
        0, count // STEP, lambda i, c: body(pl.ds(pl.multiple_of(i * STEP, STEP), STEP), i, c), init
    )


class Exchange:
    def __init__(self, n_fsdp, n_dp, send, recv, local_sem):
        self.n, self.n_dp, self.groups = n_fsdp, n_dp, n_fsdp // 2
        self.send, self.recv, self.local_sem = send, recv, local_sem
        self.count, self.local_count = 0, 0
        self.open, self.local_open = [], []
        self.me = lax.axis_index("fsdp")
        self.row = lax.axis_index("dp")
        self.core = lax.rem(self.me, 2)
        self.group = lax.div(self.me, 2)
        self.twin = {"fsdp": 2 * self.group + 1 - self.core}
        self.above = {"fsdp": lax.rem(self.me + 2, self.n)}
        self.below = {"fsdp": lax.rem(self.me + self.n - 2, self.n)}

    def dp_peer(self, k):
        return {"dp": lax.rem(self.row + k, self.n_dp)}

    def greet(self, fsdp, dp, every=False):
        targets = []
        if every:
            targets += [{"fsdp": lax.rem(self.me + k, self.n)} for k in range(1, self.n)]
        elif fsdp:
            targets += [self.twin]
            targets += [{"fsdp": lax.rem(self.me + 2 * k, self.n)} for k in range(1, self.groups)]
        if dp:
            targets += [self.dp_peer(k) for k in range(1, self.n_dp)]
        barrier = pltpu.get_barrier_semaphore()
        for device in targets:
            pl.semaphore_signal(barrier, inc=1, device_id=device, device_id_type=MESH)
        pl.semaphore_wait(barrier, len(targets))

    def plan(self, src, dst, device, when=None):
        copy = pltpu.make_async_remote_copy(
            src_ref=src,
            dst_ref=dst,
            send_sem=self.send.at[self.count],
            recv_sem=self.recv.at[self.count],
            device_id=device,
            device_id_type=MESH,
        )
        self.count += 1
        self.open.append((copy, when))
        return copy

    def start(self, src, dst, device):
        copy = self.plan(src, dst, device)
        copy.start()
        return copy

    def keep(self, src, dst):
        copy = pltpu.make_async_copy(src, dst, self.local_sem.at[self.local_count])
        copy.start()
        self.local_count += 1
        self.local_open.append(copy)

    def finish(self):
        for copy, when in self.open:
            if when is None:
                copy.wait_send()
            else:
                pl.when(when)(copy.wait_send)
        for copy in self.local_open:
            copy.wait()

    def dp_gather(self, src, dst):
        height = src.shape[0]
        place = lambda i, at, size: dst.at[pl.ds(pl.multiple_of(i * height + at, STEP), size)]
        own = place(self.row, 0, height)
        self.keep(src, own)
        if self.n_dp != 4:
            return [self.start(src, own, self.dp_peer(k)) for k in range(1, self.n_dp)], []
        across = self.row + 1 - 2 * lax.rem(self.row, 2)
        along = lax.rem(self.row + 2, 4)
        first = self.start(src, own, {"dp": across})
        second = self.start(src, own, {"dp": along})
        size = height // 2
        upper, lower = place(across, 0, size), place(along, size, size)
        return [], [
            (first, self.plan(upper, upper, {"dp": along})),
            (second, self.plan(lower, lower, {"dp": across})),
        ]

    def dp_forward(self, gather):
        direct, pairs = gather
        for arrived, onward in pairs:
            arrived.wait_recv()
            onward.start()

    def dp_close(self, gather):
        direct, pairs = gather
        for copy in direct + [onward for _, onward in pairs]:
            copy.wait_recv()

    def reduce_open(self, part, piece, twin_buf):
        order = []
        for k in range((self.groups + 1) // 2):
            order += [self.groups - 1 - k] + ([k] if k != self.groups - 1 - k else [])
        return {
            d: self.start(piece(part, 2 * d + 1 - self.core), twin_buf.at[d], self.twin)
            for d in order
        }

    def reduce_send(self, part, piece, twin_buf, half, far_buf, opened):
        g, last = self.group, self.groups - 1
        ups, downs = [], []
        for s in range(last):
            ups.append(self.plan(half.at[0, s], far_buf.at[0, s], self.above, g < last - s))
            downs.append(self.plan(half.at[1, s], far_buf.at[1, s], self.below, g > s))

        def hop(way, s):
            target = last - s if way == 0 else s
            copy = (ups if way == 0 else downs)[s]
            inner = g > 0 if way == 0 else g < last
            mine = piece(part, 2 * target + self.core)

            def add(with_far):
                def step(rows, i, c):
                    value = mine[rows, :].astype(F32) + twin_buf[target, rows, :].astype(F32)
                    if with_far:
                        value = value + far_buf[way, s, rows, :].astype(F32)
                    half[way, s, rows, :] = value.astype(BF)
                    return c

                over_rows(half.shape[2], step)

            @pl.when(g < target if way == 0 else g > target)
            def _():
                opened[target].wait_recv()

                @pl.when(inner)
                def _():
                    copy.wait_recv()
                    add(True)

                @pl.when(jnp.logical_not(inner))
                def _():
                    add(False)

                copy.start()

        @pl.when(g < self.groups // 2)
        def _():
            for s in range(last):
                hop(0, s)
                hop(1, s)

        @pl.when(g >= self.groups // 2)
        def _():
            for s in range(last):
                hop(1, s)
                hop(0, s)

        return ups, downs

    def reduce_close(self, part, piece, twin_buf, half, far_buf, opened, sent):
        g, last = self.group, self.groups - 1
        ups, downs = sent
        for d in range(self.groups):
            pl.when(g == d)(opened[d].wait_recv)
        for s in range(last):
            pl.when(jnp.logical_and(g == last - s, g > 0))(ups[s].wait_recv)
            pl.when(jnp.logical_and(g == s, g < last))(downs[s].wait_recv)
        mine = piece(part, self.me)
        from_below = jnp.clip(last - g, 0, last - 1)
        from_above = jnp.clip(g, 0, last - 1)

        def apply(store, height, init=0):
            def run(below, above):
                def step(rows, i, c):
                    value = mine[rows, :].astype(F32) + twin_buf[g, rows, :].astype(F32)
                    if below:
                        value = value + far_buf[0, from_below, rows, :].astype(F32)
                    if above:
                        value = value + far_buf[1, from_above, rows, :].astype(F32)
                    return store(value, rows, i, c)

                return over_rows(height, step, init)

            return lax.cond(
                g == 0,
                lambda: run(False, True),
                lambda: lax.cond(g == last, lambda: run(True, False), lambda: run(True, True)),
            )

        return apply

    def spread(self, own, full, piece, between=None):
        g, last = self.group, self.groups - 1
        target = piece(full, self.me)
        self.keep(own, target)
        near = [(self.start(own, target, self.twin), None)]
        hops = []
        for t in range(last):
            for way, device in ((1, self.above), (-1, self.below)):
                block = own if t == 0 else piece(full, 2 * ((g - way * t + self.groups) % self.groups) + self.core)
                there = target if t == 0 else block
                sends = jnp.logical_and(g < last, g >= t) if way == 1 else jnp.logical_and(g > 0, g + t <= last)
                gets = g >= t + 1 if way == 1 else g + t + 1 <= last
                come = piece(full, 2 * ((g - way * (t + 1) + self.groups) % self.groups) + self.core)
                hops.append((t, self.plan(block, there, device, sends), sends, gets,
                             self.plan(come, come, self.twin, gets)))
        for t in range(last):
            mine = [hop for hop in hops if hop[0] == t]
            for _, copy, sends, _, _ in mine:
                pl.when(sends)(copy.start)
            if t == 0 and between is not None:
                between()
            for _, copy, _, gets, onward in mine:

                def pass_on(copy=copy, onward=onward):
                    copy.wait_recv()
                    onward.start()

                pl.when(gets)(pass_on)
                near.append((onward, gets))

        def close():
            for copy, gets in near:
                if gets is None:
                    copy.wait_recv()
                else:
                    pl.when(gets)(copy.wait_recv)

        return close

    def sum_tiles(self, tiles, row_tiles):
        copies = [
            self.start(
                tiles.at[self.me], tiles.at[self.me], {"fsdp": lax.rem(self.me + k, self.n)}
            )
            for k in range(1, self.n)
        ]
        for copy in copies:
            copy.wait_recv()
        value = tiles[0]
        for j in range(1, self.n):
            value = value + tiles[j]
        row_tiles[self.row] = value
        copies = [
            self.start(row_tiles.at[self.row], row_tiles.at[self.row], self.dp_peer(k))
            for k in range(1, self.n_dp)
        ]
        for copy in copies:
            copy.wait_recv()
        value = row_tiles[0]
        for j in range(1, self.n_dp):
            value = value + row_tiles[j]
        return value


def reduce_scratch(n, height, width):
    g = n // 2
    return [
        pltpu.VMEM((g, height, width), BF),
        pltpu.VMEM((2, g - 1, height, width), BF),
        pltpu.VMEM((2, g - 1, height, width), BF),
    ]


def communicate(body, n, n_dp, copies, kept, outs, ins, scratch, ident, flops=0):
    sems = [
        pltpu.SemaphoreType.DMA((copies,)),
        pltpu.SemaphoreType.DMA((copies,)),
        pltpu.SemaphoreType.DMA((max(kept, 1),)),
    ]

    def kernel(*refs):
        ex = Exchange(n, n_dp, refs[-3], refs[-2], refs[-1])
        body(ex, *refs[:-3])
        ex.finish()
        assert ex.count <= copies and ex.local_count == kept, (ex.count, ex.local_count)

    vmem = pl.BlockSpec(memory_space=pltpu.VMEM)
    anyw = pl.BlockSpec(memory_space=pl.ANY)
    return pl.pallas_call(
        kernel,
        out_shape=[jax.ShapeDtypeStruct(shape, kind) for shape, kind, _ in outs],
        in_specs=[vmem if v else anyw for _, v in ins],
        out_specs=[vmem if v else anyw for _, _, v in outs],
        scratch_shapes=list(scratch) + sems,
        compiler_params=pltpu.CompilerParams(
            collective_id=ident, has_side_effects=True, vmem_limit_bytes=40 * 1024 * 1024
        ),
    )(*[a for a, _ in ins])


def forward_exchange(n, n_dp, n_tgt, part, row_cols, goal_cols, hidden):
    height, width = row_cols.shape
    piece = columns_of(width)
    tgt_share, poi_share = 1.0 / (n_tgt * n_dp), 1.0 / ((height - n_tgt) * n_dp)

    def body(ex, part, x, goal, hidden, error, own, all_x, all_h, all_e, twin, half, far):
        ex.greet(True, True)
        opened = ex.reduce_open(part, piece, twin)
        gathers = [ex.dp_gather(x, all_x), ex.dp_gather(hidden, all_h)]
        sent = ex.reduce_send(part, piece, twin, half, far, opened)
        apply = ex.reduce_close(part, piece, twin, half, far, opened, sent)

        def loss(total, rows, i, c):
            share = jnp.where(i * STEP < n_tgt, tgt_share, poi_share)
            value = x[rows, :].astype(F32) + total - goal[rows, :].astype(F32)
            own[rows, :] = (value * share).astype(BF)
            return c

        apply(loss, height)

        def between():
            for gather in gathers:
                ex.dp_forward(gather)
            gathers.append(ex.dp_gather(own, all_e))

        close = ex.spread(own, error, piece, between)
        ex.dp_forward(gathers[-1])
        close()
        for gather in gathers:
            ex.dp_close(gather)

    return communicate(
        body, n, n_dp, 6 * n + 3 * n_dp, 4,
        [
            ((height, width * n), BF, True),
            ((height, width), BF, True),
            ((height * n_dp, width), BF, False),
            ((height * n_dp, hidden.shape[1]), BF, False),
            ((height * n_dp, width), BF, False),
        ],
        [(part, True), (row_cols, True), (goal_cols, True), (hidden, False)],
        reduce_scratch(n, height, width), 1,
    )


def gram_exchange(n, n_dp, grams, back_both):
    height, width = grams.shape
    piece = rows_of(height // n)

    def body(ex, grams, back, summed, all_b, own, twin, half, far):
        ex.greet(True, True)
        opened = ex.reduce_open(grams, piece, twin)
        gather = ex.dp_gather(back, all_b)
        sent = ex.reduce_send(grams, piece, twin, half, far, opened)
        apply = ex.reduce_close(grams, piece, twin, half, far, opened, sent)

        def store(total, rows, i, c):
            own[rows, :] = total.astype(BF)
            return c

        apply(store, height // n)
        close = ex.spread(own, summed, piece, lambda: ex.dp_forward(gather))
        close()
        ex.dp_close(gather)

    return communicate(
        body, n, n_dp, 6 * n + n_dp, 2,
        [
            ((height, width), BF, True),
            ((back_both.shape[0] * n_dp, back_both.shape[1]), BF, False),
        ],
        [(grams, True), (back_both, False)],
        [pltpu.VMEM((height // n, width), BF)] + reduce_scratch(n, height // n, width), 2,
    )


def sum_exchange(n, n_dp, tile):
    def body(ex, tile, out, tiles, row_tiles):
        ex.greet(True, True, every=True)
        tiles[ex.me] = tile[...]
        out[...] = ex.sum_tiles(tiles, row_tiles)

    return communicate(
        body, n, n_dp, (n - 1) + (n_dp - 1), 0,
        [(tile.shape, F32, True)],
        [(tile, True)],
        [pltpu.VMEM((n,) + tile.shape, F32), pltpu.VMEM((n_dp,) + tile.shape, F32)], 3,
    )[0]


def tangent_exchange(n, n_dp, poi_total, part, extra, gram):
    height, width = extra.shape
    piece = columns_of(width)
    low = gram.shape[0] // n
    low_piece = rows_of(low)

    def body(ex, part, extra, gram, full, own, summed, low_own, t1, h1, f1, t2, h2, f2):
        ex.greet(True, False)
        opened = ex.reduce_open(part, piece, t1)
        low_opened = ex.reduce_open(gram, low_piece, t2)
        sent = ex.reduce_send(part, piece, t1, h1, f1, opened)
        low_sent = ex.reduce_send(gram, low_piece, t2, h2, f2, low_opened)
        apply = ex.reduce_close(part, piece, t1, h1, f1, opened, sent)

        def store(total, rows, i, c):
            own[rows, :] = ((total + extra[rows, :]) * (1.0 / poi_total)).astype(BF)
            return c

        apply(store, height)
        close = ex.spread(own, full, piece)
        low_apply = ex.reduce_close(gram, low_piece, t2, h2, f2, low_opened, low_sent)

        def low_store(total, rows, i, c):
            low_own[rows, :] = total.astype(BF)
            return c

        low_apply(low_store, low)
        low_close = ex.spread(low_own, summed, low_piece)
        close()
        low_close()

    return communicate(
        body, n, n_dp, 12 * n, 2,
        [((height, width * n), BF, True), ((height, width), BF, True), (gram.shape, BF, True)],
        [(part, True), (extra, True), (gram, True)],
        [pltpu.VMEM((low, gram.shape[1]), BF)]
        + reduce_scratch(n, height, width)
        + reduce_scratch(n, low, gram.shape[1]), 4,
    )


def final_exchange(n, n_dp, scale, entries, part, extra):
    height, width = extra.shape
    piece = columns_of(width)

    def body(ex, part, extra, out, twin, half, far, tiles, row_tiles):
        ex.greet(True, True, every=True)
        opened = ex.reduce_open(part, piece, twin)
        sent = ex.reduce_send(part, piece, twin, half, far, opened)
        apply = ex.reduce_close(part, piece, twin, half, far, opened, sent)

        def store(total, rows, i, c):
            value = (total + extra[rows, :]) * scale
            out[rows, :] = value
            return c + value * value

        squares = apply(store, height, jnp.zeros((STEP, width), F32))
        tiles[ex.me] = jnp.broadcast_to(jnp.sum(squares), (8, 128))
        summed = ex.sum_tiles(tiles, row_tiles)
        factor = lax.rsqrt(jnp.max(summed) / entries + EPSILON)

        def rescale(rows, i, c):
            out[rows, :] = out[rows, :] * factor
            return c

        over_rows(height, rescale)

    return communicate(
        body, n, n_dp, 4 * n + n_dp, 0,
        [((height, width), F32, True)],
        [(part, True), (extra, True)],
        reduce_scratch(n, height, width)
        + [pltpu.VMEM((n, 8, 128), F32), pltpu.VMEM((n_dp, 8, 128), F32)], 5,
    )[0]


def silu_parts(preact):
    sigma = jax.nn.sigmoid(preact)
    silu_val = preact * sigma
    slope = sigma * (1.0 + preact * (1.0 - sigma))
    curve = sigma * (1.0 - sigma) * (2.0 + preact * (1.0 - 2.0 * sigma))
    return (silu_val, slope, curve)


def matmul(left, right):
    return jnp.dot(left, right, preferred_element_type=F32)


def inner_cols(left, right):
    return lax.dot_general(
        left, right, (((1,), (1,)), ((), ())), preferred_element_type=F32
    )


def local(target_x, target_y, poison_x, poison_y, w_gate, w_up, w_down):
    model_width = w_gate.shape[0]
    hidden_width = w_gate.shape[1]
    n_dp = lax.axis_size("dp")
    n_fsdp = lax.axis_size("fsdp")
    n_tgt = target_x.shape[0]
    n_poi = poison_x.shape[0]
    n_row = n_tgt + n_poi
    tgt_total = n_tgt * n_dp
    poi_total = n_poi * n_dp
    columns = model_width // n_fsdp
    first = lax.axis_index("fsdp") * columns

    def own_cols(rows):
        return lax.dynamic_slice_in_dim(rows, first, columns, 1)

    is_tgt_all = (jnp.arange(n_row * n_dp) % n_row) < n_tgt

    rows = jnp.concatenate([target_x, poison_x], axis=0)
    row_cols = own_cols(rows)
    goal_cols = jnp.concatenate([own_cols(target_y), own_cols(poison_y)], axis=0)

    gate_pre = matmul(rows, w_gate)
    upper = matmul(rows, w_up)
    silu_val, slope, curve = silu_parts(gate_pre)
    hidden = (silu_val * upper).astype(BF)
    part_out = matmul(hidden, w_down).astype(BF)
    error, error_cols, all_cols, hidden_all, error_all = forward_exchange(
        n_fsdp, n_dp, n_tgt, part_out, row_cols, goal_cols, hidden
    )

    back = inner_cols(error, w_down)
    back_both = jnp.concatenate([back * upper * slope, back * silu_val], axis=1).astype(BF)
    gram_e_part = inner_cols(error_cols, error_all)
    grams, back_all = gram_exchange(
        n_fsdp,
        n_dp,
        jnp.concatenate(
            [
                inner_cols(row_cols, all_cols).astype(BF),
                inner_cols(hidden, hidden_all).astype(BF),
                gram_e_part[n_tgt:].astype(BF),
            ],
            axis=0,
        ),
        back_both,
    )
    gram_x, gram_h, gram_e = grams[:n_row], grams[n_row : 2 * n_row], grams[2 * n_row :]
    gram_b_part = inner_cols(back_both, back_all)

    both = gram_x.astype(F32) * gram_b_part + gram_h.astype(F32) * gram_e_part
    sum_tgt = jnp.sum(jnp.where(is_tgt_all[None, :], both, 0.0), axis=1)
    sum_poi = jnp.sum(jnp.where(is_tgt_all[None, :], 0.0, both), axis=1)
    sums = jnp.stack(
        [jnp.sum(sum_tgt[:n_tgt]), jnp.sum(sum_poi[n_tgt:]), jnp.sum(sum_tgt[n_tgt:])]
    )
    tile = jnp.broadcast_to(jnp.pad(sums, (0, 5))[:, None], (8, 128))
    sums = sum_exchange(n_fsdp, n_dp, tile)[:, 0]
    norm_tt, norm_pp, cross_tp = sums[0], sums[1], sums[2]
    length_tgt = jnp.sqrt(norm_tt + EPSILON)
    length_poi = jnp.sqrt(norm_pp + EPSILON)
    denom = length_tgt * length_poi
    alignment = 1.0 - cross_tp / denom
    coef_tgt = -1.0 / denom
    coef_poi = cross_tp / (denom * length_poi * length_poi)
    coef = jnp.where(is_tgt_all, coef_tgt, coef_poi)[None, :]

    def weigh(gram):
        return (gram.astype(F32) * coef).astype(BF)

    u_poi, s_poi = upper[n_tgt:], silu_val[n_tgt:]
    s1_poi, s2_poi = slope[n_tgt:], curve[n_tgt:]
    b_poi = back[n_tgt:]
    tangents = matmul(weigh(gram_x[n_tgt:]), back_all)
    tan_gate = tangents[:, :hidden_width]
    tan_upper = tangents[:, hidden_width:]
    hidden_tan = (s1_poi * tan_gate * u_poi + s_poi * tan_upper).astype(BF)
    back_tan, back_tan_cols, gram_b = tangent_exchange(
        n_fsdp,
        n_dp,
        poi_total,
        matmul(hidden_tan, w_down).astype(BF),
        matmul(weigh(gram_h[n_tgt:]), error_all),
        gram_b_part[n_tgt:].astype(BF),
    )
    mixed = inner_cols(back_tan, w_down) + matmul(weigh(gram_e), hidden_all)
    gate_total = (
        mixed * u_poi * s1_poi + b_poi * (s2_poi * tan_gate * u_poi + s1_poi * tan_upper)
    ).astype(BF)
    upper_total = (mixed * s_poi + b_poi * s1_poi * tan_gate).astype(BF)
    part_grad = inner_cols(gate_total, w_gate) + inner_cols(upper_total, w_up)
    step = final_exchange(
        n_fsdp,
        n_dp,
        float(poi_total * model_width),
        float(poi_total * model_width),
        part_grad.astype(BF),
        matmul(weigh(gram_b), all_cols) + back_tan_cols.astype(F32),
    )
    return (step, alignment)


def solution(mesh):
    in_specs = (
        P("dp", None),
        P("dp", None),
        P("dp", None),
        P("dp", None),
        P(None, "fsdp"),
        P(None, "fsdp"),
        P("fsdp", None),
    )
    out_specs = (P("dp", "fsdp"), P())
    return jax.shard_map(local, mesh=mesh, in_specs=in_specs, out_specs=out_specs, check_vma=False)
```

```python
import functools
import jax
import jax.numpy as jnp
from jax import lax
from jax.experimental import pallas as pl
from jax.experimental.pallas import tpu as pltpu
from jax.sharding import PartitionSpec as P

EPSILON = 1e-06
BF = jnp.bfloat16
F32 = jnp.float32

MESH = pl.DeviceIdType.MESH
STEP = 16


def columns_of(width):
    return lambda ref, i: ref.at[:, pl.ds(pl.multiple_of(i * width, width), width)]


def rows_of(height):
    return lambda ref, i: ref.at[pl.ds(pl.multiple_of(i * height, height), height)]


def over_rows(count, body, init=0):
    size = next(size for size in (64, 32, STEP) if count % size == 0)
    return lax.fori_loop(
        0,
        count // size,
        lambda i, c: body(pl.ds(pl.multiple_of(i * size, size), size), i * size, c),
        init,
    )


class Exchange:
    def __init__(self, n_fsdp, n_dp, send, recv, local_sem):
        self.n, self.n_dp, self.groups = n_fsdp, n_dp, n_fsdp // 2
        self.send, self.recv, self.local_sem = send, recv, local_sem
        self.count, self.local_count = 0, 0
        self.open, self.local_open = [], []
        self.me = lax.axis_index("fsdp")
        self.row = lax.axis_index("dp")
        self.core = lax.rem(self.me, 2)
        self.group = lax.div(self.me, 2)
        self.twin = {"fsdp": 2 * self.group + 1 - self.core}
        self.above = {"fsdp": lax.rem(self.me + 2, self.n)}
        self.below = {"fsdp": lax.rem(self.me + self.n - 2, self.n)}

    def dp_peer(self, k):
        return {"dp": lax.rem(self.row + k, self.n_dp)}

    def greet(self, fsdp, dp, every=False):
        targets = []
        if every:
            targets += [{"fsdp": lax.rem(self.me + k, self.n)} for k in range(1, self.n)]
        elif fsdp:
            targets += [self.twin]
            targets += [{"fsdp": lax.rem(self.me + 2 * k, self.n)} for k in range(1, self.groups)]
        if dp:
            targets += [self.dp_peer(k) for k in range(1, self.n_dp)]
        barrier = pltpu.get_barrier_semaphore()
        for device in targets:
            pl.semaphore_signal(barrier, inc=1, device_id=device, device_id_type=MESH)
        pl.semaphore_wait(barrier, len(targets))

    def plan(self, src, dst, device, when=None):
        copy = pltpu.make_async_remote_copy(
            src_ref=src,
            dst_ref=dst,
            send_sem=self.send.at[self.count],
            recv_sem=self.recv.at[self.count],
            device_id=device,
            device_id_type=MESH,
        )
        self.count += 1
        self.open.append((copy, when))
        return copy

    def start(self, src, dst, device):
        copy = self.plan(src, dst, device)
        copy.start()
        return copy

    def keep(self, src, dst):
        copy = pltpu.make_async_copy(src, dst, self.local_sem.at[self.local_count])
        copy.start()
        self.local_count += 1
        self.local_open.append(copy)

    def finish(self):
        for copy, when in self.open:
            if when is None:
                copy.wait_send()
            else:
                pl.when(when)(copy.wait_send)
        for copy in self.local_open:
            copy.wait()

    def dp_gather(self, src, dst):
        height = src.shape[0]
        place = lambda i, at, size: dst.at[pl.ds(pl.multiple_of(i * height + at, STEP), size)]
        own = place(self.row, 0, height)
        self.keep(src, own)
        if self.n_dp != 4:
            return [self.start(src, own, self.dp_peer(k)) for k in range(1, self.n_dp)], []
        across = self.row + 1 - 2 * lax.rem(self.row, 2)
        along = lax.rem(self.row + 2, 4)
        first = self.start(src, own, {"dp": across})
        second = self.start(src, own, {"dp": along})
        size = height // 2
        upper, lower = place(across, 0, size), place(along, size, size)
        return [], [
            (first, self.plan(upper, upper, {"dp": along})),
            (second, self.plan(lower, lower, {"dp": across})),
        ]

    def dp_forward(self, gather):
        direct, pairs = gather
        for arrived, onward in pairs:
            arrived.wait_recv()
            onward.start()

    def dp_close(self, gather):
        direct, pairs = gather
        for copy in direct + [onward for _, onward in pairs]:
            copy.wait_recv()

    def reduce_open(self, part, piece, twin_buf):
        order = []
        for k in range((self.groups + 1) // 2):
            order += [self.groups - 1 - k] + ([k] if k != self.groups - 1 - k else [])
        return {
            d: self.start(piece(part, 2 * d + 1 - self.core), twin_buf.at[d], self.twin)
            for d in order
        }

    def reduce_send(self, part, piece, twin_buf, half, far_buf, opened):
        g, last = self.group, self.groups - 1
        ups, downs = [], []
        for s in range(last):
            ups.append(self.plan(half.at[0, s], far_buf.at[0, s], self.above, g < last - s))
            downs.append(self.plan(half.at[1, s], far_buf.at[1, s], self.below, g > s))

        def hop(way, s):
            target = last - s if way == 0 else s
            copy = (ups if way == 0 else downs)[s]
            inner = g > 0 if way == 0 else g < last
            mine = piece(part, 2 * target + self.core)

            def add(with_far):
                def step(rows, i, c):
                    value = mine[rows, :].astype(F32) + twin_buf[target, rows, :].astype(F32)
                    if with_far:
                        value = value + far_buf[way, s, rows, :].astype(F32)
                    half[way, s, rows, :] = value.astype(BF)
                    return c

                over_rows(half.shape[2], step)

            @pl.when(g < target if way == 0 else g > target)
            def _():
                opened[target].wait_recv()

                @pl.when(inner)
                def _():
                    copy.wait_recv()
                    add(True)

                @pl.when(jnp.logical_not(inner))
                def _():
                    add(False)

                copy.start()

        @pl.when(g < self.groups // 2)
        def _():
            for s in range(last):
                hop(0, s)
                hop(1, s)

        @pl.when(g >= self.groups // 2)
        def _():
            for s in range(last):
                hop(1, s)
                hop(0, s)

        return ups, downs

    def reduce_close(self, part, piece, twin_buf, half, far_buf, opened, sent):
        g, last = self.group, self.groups - 1
        ups, downs = sent
        for d in range(self.groups):
            pl.when(g == d)(opened[d].wait_recv)
        for s in range(last):
            pl.when(jnp.logical_and(g == last - s, g > 0))(ups[s].wait_recv)
            pl.when(jnp.logical_and(g == s, g < last))(downs[s].wait_recv)
        mine = piece(part, self.me)
        from_below = jnp.clip(last - g, 0, last - 1)
        from_above = jnp.clip(g, 0, last - 1)

        def apply(store, height, init=0):
            def run(below, above):
                def step(rows, i, c):
                    value = mine[rows, :].astype(F32) + twin_buf[g, rows, :].astype(F32)
                    if below:
                        value = value + far_buf[0, from_below, rows, :].astype(F32)
                    if above:
                        value = value + far_buf[1, from_above, rows, :].astype(F32)
                    return store(value, rows, i, c)

                return over_rows(height, step, init)

            return lax.cond(
                g == 0,
                lambda: run(False, True),
                lambda: lax.cond(g == last, lambda: run(True, False), lambda: run(True, True)),
            )

        return apply

    def spread(self, own, full, piece, between=None):
        g, last = self.group, self.groups - 1
        target = piece(full, self.me)
        self.keep(own, target)
        near = []
        hops = []
        for t in range(last):
            for way, device in ((1, self.above), (-1, self.below)):
                block = own if t == 0 else piece(full, 2 * ((g - way * t + self.groups) % self.groups) + self.core)
                there = target if t == 0 else block
                sends = jnp.logical_and(g < last, g >= t) if way == 1 else jnp.logical_and(g > 0, g + t <= last)
                gets = g >= t + 1 if way == 1 else g + t + 1 <= last
                come = piece(full, 2 * ((g - way * (t + 1) + self.groups) % self.groups) + self.core)
                hops.append((t, self.plan(block, there, device, sends), sends, gets,
                             self.plan(come, come, self.twin, gets)))
        for t in range(last):
            mine = [hop for hop in hops if hop[0] == t]
            for _, copy, sends, _, _ in mine:
                pl.when(sends)(copy.start)
            if t == 0:
                near.append((self.start(own, target, self.twin), None))
            if t == 0 and between is not None:
                between()
            for _, copy, _, gets, onward in mine:

                def pass_on(copy=copy, onward=onward):
                    copy.wait_recv()
                    onward.start()

                pl.when(gets)(pass_on)
                near.append((onward, gets))

        def close():
            for copy, gets in near:
                if gets is None:
                    copy.wait_recv()
                else:
                    pl.when(gets)(copy.wait_recv)

        return close

    def sum_tiles(self, tiles, row_tiles):
        copies = [
            self.start(
                tiles.at[self.me], tiles.at[self.me], {"fsdp": lax.rem(self.me + k, self.n)}
            )
            for k in range(1, self.n)
        ]
        for copy in copies:
            copy.wait_recv()
        value = tiles[0]
        for j in range(1, self.n):
            value = value + tiles[j]
        row_tiles[self.row] = value
        copies = [
            self.start(row_tiles.at[self.row], row_tiles.at[self.row], self.dp_peer(k))
            for k in range(1, self.n_dp)
        ]
        for copy in copies:
            copy.wait_recv()
        value = row_tiles[0]
        for j in range(1, self.n_dp):
            value = value + row_tiles[j]
        return value


def reduce_scratch(n, height, width):
    g = n // 2
    return [
        pltpu.VMEM((g, height, width), BF),
        pltpu.VMEM((2, g - 1, height, width), BF),
        pltpu.VMEM((2, g - 1, height, width), BF),
    ]


def communicate(body, n, n_dp, copies, kept, outs, ins, scratch, ident, flops=0):
    sems = [
        pltpu.SemaphoreType.DMA((copies,)),
        pltpu.SemaphoreType.DMA((copies,)),
        pltpu.SemaphoreType.DMA((max(kept, 1),)),
    ]

    def kernel(*refs):
        ex = Exchange(n, n_dp, refs[-3], refs[-2], refs[-1])
        body(ex, *refs[:-3])
        ex.finish()
        assert ex.count <= copies and ex.local_count == kept, (ex.count, ex.local_count)

    vmem = pl.BlockSpec(memory_space=pltpu.VMEM)
    anyw = pl.BlockSpec(memory_space=pl.ANY)
    return pl.pallas_call(
        kernel,
        out_shape=[jax.ShapeDtypeStruct(shape, kind) for shape, kind, _ in outs],
        in_specs=[vmem if v else anyw for _, v in ins],
        out_specs=[vmem if v else anyw for _, _, v in outs],
        scratch_shapes=list(scratch) + sems,
        compiler_params=pltpu.CompilerParams(
            collective_id=ident, has_side_effects=True, vmem_limit_bytes=40 * 1024 * 1024
        ),
    )(*[a for a, _ in ins])


def forward_exchange(n, n_dp, n_tgt, part, row_cols, goal_cols, hidden):
    height, width = row_cols.shape
    piece = columns_of(width)
    tgt_share, poi_share = 1.0 / (n_tgt * n_dp), 1.0 / ((height - n_tgt) * n_dp)

    def body(ex, part, x, goal, hidden, error, own, all_x, all_h, all_e, twin, half, far):
        ex.greet(True, True)
        opened = ex.reduce_open(part, piece, twin)
        gathers = [ex.dp_gather(x, all_x), ex.dp_gather(hidden, all_h)]
        sent = ex.reduce_send(part, piece, twin, half, far, opened)
        apply = ex.reduce_close(part, piece, twin, half, far, opened, sent)

        def loss(total, rows, i, c):
            share = jnp.where(i < n_tgt, tgt_share, poi_share)
            value = x[rows, :].astype(F32) + total - goal[rows, :].astype(F32)
            own[rows, :] = (value * share).astype(BF)
            return c

        apply(loss, height)

        def between():
            for gather in gathers:
                ex.dp_forward(gather)
            gathers.append(ex.dp_gather(own, all_e))

        close = ex.spread(own, error, piece, between)
        ex.dp_forward(gathers[-1])
        close()
        for gather in gathers:
            ex.dp_close(gather)

    return communicate(
        body, n, n_dp, 6 * n + 3 * n_dp, 4,
        [
            ((height, width * n), BF, True),
            ((height, width), BF, True),
            ((height * n_dp, width), BF, False),
            ((height * n_dp, hidden.shape[1]), BF, False),
            ((height * n_dp, width), BF, False),
        ],
        [(part, True), (row_cols, True), (goal_cols, True), (hidden, False)],
        reduce_scratch(n, height, width), 1,
    )


def gram_exchange(n, n_dp, grams, back_both):
    height, width = grams.shape
    piece = rows_of(height // n)

    def body(ex, grams, back, summed, all_b, own, twin, half, far):
        ex.greet(True, True)
        opened = ex.reduce_open(grams, piece, twin)
        gather = ex.dp_gather(back, all_b)
        sent = ex.reduce_send(grams, piece, twin, half, far, opened)
        apply = ex.reduce_close(grams, piece, twin, half, far, opened, sent)

        def store(total, rows, i, c):
            own[rows, :] = total.astype(BF)
            return c

        apply(store, height // n)
        close = ex.spread(own, summed, piece, lambda: ex.dp_forward(gather))
        close()
        ex.dp_close(gather)

    return communicate(
        body, n, n_dp, 6 * n + n_dp, 2,
        [
            ((height, width), BF, True),
            ((back_both.shape[0] * n_dp, back_both.shape[1]), BF, False),
        ],
        [(grams, True), (back_both, False)],
        [pltpu.VMEM((height // n, width), BF)] + reduce_scratch(n, height // n, width), 2,
    )


def coef_exchange(n, n_dp, n_tgt, with_tgt, with_poi):
    split = n_tgt // 128

    def body(ex, with_tgt, with_poi, out, tiles, row_tiles):
        ex.greet(True, True, every=True)
        tiles[ex.me] = jnp.concatenate(
            [
                jnp.sum(with_tgt[:split], axis=0, keepdims=True),
                jnp.sum(with_poi[split:], axis=0, keepdims=True),
                jnp.sum(with_tgt[split:], axis=0, keepdims=True),
                jnp.zeros((5, 128), F32),
            ],
            axis=0,
        )
        sums = jnp.sum(ex.sum_tiles(tiles, row_tiles), axis=1, keepdims=True)
        sums = jnp.broadcast_to(sums, (8, 128))
        length_tgt = jnp.sqrt(sums[0:1] + EPSILON)
        length_poi = jnp.sqrt(sums[1:2] + EPSILON)
        denom = length_tgt * length_poi
        cross = sums[2:3]
        out[0:1] = -1.0 / denom
        out[1:2] = cross / (denom * length_poi * length_poi)
        out[2:3] = 1.0 - cross / denom
        out[3:8] = jnp.zeros((5, 128), F32)

    return communicate(
        body, n, n_dp, (n - 1) + (n_dp - 1), 0,
        [((8, 128), F32, True)],
        [(with_tgt, True), (with_poi, True)],
        [pltpu.VMEM((n, 8, 128), F32), pltpu.VMEM((n_dp, 8, 128), F32)], 3,
    )[0]


def tangent_exchange(n, n_dp, poi_total, part, extra, gram):
    height, width = extra.shape
    piece = columns_of(width)
    low = gram.shape[0] // n
    low_piece = rows_of(low)

    def body(ex, part, extra, gram, full, own, summed, low_own, t1, h1, f1, t2, h2, f2):
        ex.greet(True, False)
        opened = ex.reduce_open(part, piece, t1)
        low_opened = ex.reduce_open(gram, low_piece, t2)
        sent = ex.reduce_send(part, piece, t1, h1, f1, opened)
        low_sent = ex.reduce_send(gram, low_piece, t2, h2, f2, low_opened)
        apply = ex.reduce_close(part, piece, t1, h1, f1, opened, sent)

        def store(total, rows, i, c):
            own[rows, :] = ((total + extra[rows, :]) * (1.0 / poi_total)).astype(BF)
            return c

        apply(store, height)
        close = ex.spread(own, full, piece)
        low_apply = ex.reduce_close(gram, low_piece, t2, h2, f2, low_opened, low_sent)

        def low_store(total, rows, i, c):
            low_own[rows, :] = total.astype(BF)
            return c

        low_apply(low_store, low)
        low_close = ex.spread(low_own, summed, low_piece)
        close()
        low_close()

    return communicate(
        body, n, n_dp, 12 * n, 2,
        [((height, width * n), BF, True), ((height, width), BF, True), (gram.shape, BF, True)],
        [(part, True), (extra, True), (gram, True)],
        [pltpu.VMEM((low, gram.shape[1]), BF)]
        + reduce_scratch(n, height, width)
        + reduce_scratch(n, low, gram.shape[1]), 4,
    )


def final_exchange(n, n_dp, scale, entries, part, extra):
    height, width = extra.shape
    piece = columns_of(width)

    def body(ex, part, extra, out, twin, half, far, tiles, row_tiles):
        ex.greet(True, True, every=True)
        opened = ex.reduce_open(part, piece, twin)
        sent = ex.reduce_send(part, piece, twin, half, far, opened)
        apply = ex.reduce_close(part, piece, twin, half, far, opened, sent)

        def store(total, rows, i, c):
            value = (total + extra[rows, :]) * scale
            out[rows, :] = value
            return c + jnp.sum((value * value).reshape(-1, 8, width), axis=0)

        squares = apply(store, height, jnp.zeros((8, width), F32))
        tiles[ex.me] = jnp.broadcast_to(jnp.sum(squares), (8, 128))
        summed = ex.sum_tiles(tiles, row_tiles)
        factor = lax.rsqrt(jnp.max(summed) / entries + EPSILON)

        def rescale(rows, i, c):
            out[rows, :] = out[rows, :] * factor
            return c

        over_rows(height, rescale)

    return communicate(
        body, n, n_dp, 4 * n + n_dp, 0,
        [((height, width), F32, True)],
        [(part, True), (extra, True)],
        reduce_scratch(n, height, width)
        + [pltpu.VMEM((n, 8, 128), F32), pltpu.VMEM((n_dp, 8, 128), F32)], 5,
    )[0]


def silu_parts(preact):
    sigma = jax.nn.sigmoid(preact)
    silu_val = preact * sigma
    slope = sigma * (1.0 + preact * (1.0 - sigma))
    curve = sigma * (1.0 - sigma) * (2.0 + preact * (1.0 - 2.0 * sigma))
    return (silu_val, slope, curve)


def matmul(left, right):
    return jnp.dot(left, right, preferred_element_type=F32)


def inner_cols(left, right):
    return lax.dot_general(
        left, right, (((1,), (1,)), ((), ())), preferred_element_type=F32
    )


def local(target_x, target_y, poison_x, poison_y, w_gate, w_up, w_down):
    model_width = w_gate.shape[0]
    hidden_width = w_gate.shape[1]
    n_dp = lax.axis_size("dp")
    n_fsdp = lax.axis_size("fsdp")
    n_tgt = target_x.shape[0]
    n_poi = poison_x.shape[0]
    n_row = n_tgt + n_poi
    tgt_total = n_tgt * n_dp
    poi_total = n_poi * n_dp
    columns = model_width // n_fsdp
    first = lax.axis_index("fsdp") * columns

    def own_cols(rows):
        return lax.dynamic_slice_in_dim(rows, first, columns, 1)

    is_tgt_all = (jnp.arange(n_row * n_dp) % n_row) < n_tgt

    rows = jnp.concatenate([target_x, poison_x], axis=0)
    row_cols = own_cols(rows)
    goal_cols = jnp.concatenate([own_cols(target_y), own_cols(poison_y)], axis=0)

    gate_pre = matmul(rows, w_gate)
    upper = matmul(rows, w_up)
    silu_val, slope, curve = silu_parts(gate_pre)
    hidden = (silu_val * upper).astype(BF)
    part_out = matmul(hidden, w_down).astype(BF)
    error, error_cols, all_cols, hidden_all, error_all = forward_exchange(
        n_fsdp, n_dp, n_tgt, part_out, row_cols, goal_cols, hidden
    )

    back = inner_cols(error, w_down)
    back_both = jnp.concatenate([back * upper * slope, back * silu_val], axis=1).astype(BF)
    gram_e_part = inner_cols(error_cols, error_all)
    grams, back_all = gram_exchange(
        n_fsdp,
        n_dp,
        jnp.concatenate(
            [
                inner_cols(row_cols, all_cols).astype(BF),
                inner_cols(hidden, hidden_all).astype(BF),
                gram_e_part[n_tgt:].astype(BF),
            ],
            axis=0,
        ),
        back_both,
    )
    gram_x, gram_h, gram_e = grams[:n_row], grams[n_row : 2 * n_row], grams[2 * n_row :]
    gram_b_part = inner_cols(back_both, back_all)

    both = gram_x.astype(F32) * gram_b_part + gram_h.astype(F32) * gram_e_part
    sum_tgt = jnp.sum(jnp.where(is_tgt_all[None, :], both, 0.0), axis=1)
    sum_poi = jnp.sum(jnp.where(is_tgt_all[None, :], 0.0, both), axis=1)
    coefs = coef_exchange(
        n_fsdp, n_dp, n_tgt, sum_tgt.reshape(-1, 128), sum_poi.reshape(-1, 128)
    )
    alignment = coefs[2, 0]
    coef = jnp.where(is_tgt_all, coefs[0, 0], coefs[1, 0])[None, :]

    def weigh(gram):
        return (gram.astype(F32) * coef).astype(BF)

    u_poi, s_poi = upper[n_tgt:], silu_val[n_tgt:]
    s1_poi, s2_poi = slope[n_tgt:], curve[n_tgt:]
    b_poi = back[n_tgt:]
    tangents = matmul(weigh(gram_x[n_tgt:]), back_all)
    tan_gate = tangents[:, :hidden_width]
    tan_upper = tangents[:, hidden_width:]
    hidden_tan = (s1_poi * tan_gate * u_poi + s_poi * tan_upper).astype(BF)
    back_tan, back_tan_cols, gram_b = tangent_exchange(
        n_fsdp,
        n_dp,
        poi_total,
        matmul(hidden_tan, w_down).astype(BF),
        matmul(weigh(gram_h[n_tgt:]), error_all),
        gram_b_part[n_tgt:].astype(BF),
    )
    mixed = inner_cols(back_tan, w_down) + matmul(weigh(gram_e), hidden_all)
    gate_total = (
        mixed * u_poi * s1_poi + b_poi * (s2_poi * tan_gate * u_poi + s1_poi * tan_upper)
    ).astype(BF)
    upper_total = (mixed * s_poi + b_poi * s1_poi * tan_gate).astype(BF)
    part_grad = inner_cols(gate_total, w_gate) + inner_cols(upper_total, w_up)
    step = final_exchange(
        n_fsdp,
        n_dp,
        float(poi_total * model_width),
        float(poi_total * model_width),
        part_grad.astype(BF),
        matmul(weigh(gram_b), all_cols) + back_tan_cols.astype(F32),
    )
    return (step, alignment)


def solution(mesh):
    in_specs = (
        P("dp", None),
        P("dp", None),
        P("dp", None),
        P("dp", None),
        P(None, "fsdp"),
        P(None, "fsdp"),
        P("fsdp", None),
    )
    out_specs = (P("dp", "fsdp"), P())
    return jax.shard_map(local, mesh=mesh, in_specs=in_specs, out_specs=out_specs, check_vma=False)
```
